256 devices in a mesh: row: 4 (over x_lo, core), ang: 64 (over y, x_hi, z).
Axes of the slice: x: 4 (x_hi: 2, x_lo: 2; x = x_hi * 2 + x_lo), y: 4, z: 8, core: 2. Of those that a mesh axis runs over, the one named last changes fastest.
Arguments:
- linv_t: bfloat16 [2, 2048, 2048], P(None, 'ang', 'row'), may hold values from -1.5 to 1.5, as said below
- rhs_top: float32 [2, 2048, 32768], P(None, 'row', 'ang'), may hold values from -6 to 6
- factor_t: bfloat16 [2, 2048, 4096], P(None, 'ang', 'row'), may hold values from -0.125 to 0.125
- rhs_rest: float32 [2, 4096, 32768], P(None, 'row', 'ang'), may hold values from -6 to 6
Outputs:
- solved: float32 [2, 2048, 32768], P(None, 'row', 'ang')
- updated: float32 [2, 4096, 32768], P(None, 'row', 'ang')
The draws below stay inside these ranges and needn't reach their ends.
Inputs may be any that keep to these rules, and one draw needn't show every extreme that they name: `linv_t`: lower triangular inverse: entry [c, j, i] is zero where j > i; the diagonal is real and between 0.5 and 1.5.
All inputs are finite; a program needn't handle non-finite values.
Results may differ from the reference program's by a relative error of at most 0.0026.
Values may be sent and summed in bfloat16 or wider, within the bound.
No kernel may reach another device: no remote copies, remote signals or barrier semaphores. Data moves between devices by JAX's collectives and lax.ppermute only.
A program may use at most 128 MiB of HBM per device.

```python
import math
import jax
import jax.numpy as jnp
from jax import lax

PANEL = 2048
ANG_DEV = 512
TRAIL = 4096
ANGLES = 32768
N_ANG = 64


def draw_linv_t(key, part):
    first_key, second_key = jax.random.split(jax.random.fold_in(key, 17))
    spread = jax.random.normal(first_key, (2, PANEL, PANEL), jnp.float32)
    spread = spread * (0.7 / math.sqrt(PANEL))
    col_index = lax.broadcasted_iota(jnp.int32, (PANEL, PANEL), 0)
    row_index = lax.broadcasted_iota(jnp.int32, (PANEL, PANEL), 1)
    lower = (col_index < row_index).astype(jnp.float32)
    diag_vals = jax.random.uniform(second_key, (PANEL,), jnp.float32, 0.5, 1.5)
    eye_part = (col_index == row_index).astype(jnp.float32) * diag_vals[None, :]
    real_part = spread[0] * lower + eye_part
    imag_part = spread[1] * lower
    return jnp.stack([real_part, imag_part]).astype(jnp.bfloat16)


def steps_of(key, shape, cuts, least, largest):
    level, own = 1.0, jax.random.fold_in(key, 6)
    for position, shards_of in cuts:
        heights = jnp.exp(jax.random.uniform(jax.random.fold_in(own, position), (shards_of,), jnp.float32, least / len(cuts), largest / len(cuts)))
        level = level * jnp.repeat(heights, shape[position] // shards_of).reshape([-1 if axis == position else 1 for axis in range(len(shape))])
    return level


def normal_values(key, shape, scale, most, cuts=(), held_as=jnp.bfloat16):
    array = jax.random.normal(key, shape, jnp.float32) * scale
    if len(cuts) > 0:
        array = steps_of(key, shape, cuts, -0.22, 0.18) * array
    return jnp.clip(array, min=-most, max=most).astype(held_as)


def setup_inputs(seed: int = 0) -> dict:
    keys = jax.random.split(jax.random.key(seed), 5)
    return {
        "linv_t": draw_linv_t(jax.random.fold_in(keys[4], 71), 0),
        "rhs_top": normal_values(keys[1], (2, PANEL, ANGLES), 1.0, 6.0, ((1, 4), (2, 64)), jnp.float32),
        "factor_t": normal_values(keys[2], (2, PANEL, TRAIL), PANEL ** -0.5, 0.125, ((1, 64), (2, 4))),
        "rhs_rest": normal_values(keys[3], (2, TRAIL, ANGLES), 1.0, 6.0, ((1, 4), (2, 64)), jnp.float32),
    }


def complex_tdot(left, right, precision):
    dims = (((0,), (0,)), ((), ()))

    def single(first, second):
        return lax.dot_general(first, second, dims, precision=precision, preferred_element_type=jnp.float32)

    real_part = single(left[0], right[0]) - single(left[1], right[1])
    imag_part = single(left[0], right[1]) + single(left[1], right[0])
    return jnp.stack([real_part, imag_part])


def reference(linv_t, rhs_top, factor_t, rhs_rest):
    inverse = linv_t.astype(jnp.float32)
    blocks = N_ANG

    def per_block(index):
        top_block = lax.dynamic_slice_in_dim(rhs_top, index * ANG_DEV, ANG_DEV, 2)
        rest_block = lax.dynamic_slice_in_dim(rhs_rest, index * ANG_DEV, ANG_DEV, 2)
        solved = complex_tdot(inverse, top_block, lax.Precision.HIGHEST)
        update = complex_tdot(factor_t, solved.astype(jnp.bfloat16), None)
        return solved, rest_block - update

    solved_blocks, rest_blocks = lax.map(per_block, jnp.arange(blocks, dtype=jnp.int32))
    solved = jnp.moveaxis(solved_blocks, 0, 2).reshape(2, rhs_top.shape[1], rhs_top.shape[2])
    updated = jnp.moveaxis(rest_blocks, 0, 2).reshape(2, rhs_rest.shape[1], rhs_rest.shape[2])
    return solved, updated
```

```python
import math

import jax
import jax.numpy as jnp
from jax import lax
from jax.experimental import pallas as pl
from jax.experimental.pallas import tpu as pltpu
from jax.sharding import Mesh
from jax.sharding import PartitionSpec as P

L_A = 256
F_A = 512


def after(value, *earlier):
    return lax.optimization_barrier((value, *earlier))[0]


def shift(value, axis, step):
    n = lax.axis_size(axis)
    return lax.ppermute(value, axis, [(i, (i + step) % n) for i in range(n)])


def laid_out(pieces, dim, places):
    first = pieces[0]
    shape = (*first.shape[:dim], len(pieces), *first.shape[dim:])
    lead = (slice(None),) * dim

    def kernel(*refs):
        out = refs[len(pieces)]
        for i, at in enumerate(places()):
            out[(*lead, at)] = refs[i][...]

    size = 2 * math.prod(shape) * first.dtype.itemsize
    return pl.pallas_call(
        kernel,
        out_shape=jax.ShapeDtypeStruct(shape, first.dtype),
        in_specs=[pl.BlockSpec(memory_space=pltpu.VMEM)] * len(pieces),
        out_specs=pl.BlockSpec(memory_space=pltpu.VMEM),
        compiler_params=pltpu.CompilerParams(vmem_limit_bytes=16 << 20),
        cost_estimate=pl.CostEstimate(flops=0, bytes_accessed=size, transcendentals=0),
    )(*pieces)


def row_distance():
    r = 2 * lax.axis_index("xl") + lax.axis_index("core")
    y = lax.axis_index("y")
    return [r ^ lax.rem(y + o, 4) for o in range(4)]


def along_z():
    z = lax.axis_index("z")
    return [lax.rem(z + o, 8) for o in range(8)]


def ring(value, axis, far_up, holds=None):
    n = lax.axis_size(axis)
    held = {0: value}
    for k in range(1, n // 2 + 1):
        up, down = held[(n - k + 1) % n], held[k - 1]
        if k > 1:
            extra = () if holds is None else holds.get(k, ())
            up, down = lax.optimization_barrier((up, down, *extra))[:2]
        if k < n // 2 or far_up:
            held[n - k] = shift(up, axis, 1)
        if k < n // 2 or not far_up:
            held[k] = shift(down, axis, -1)
    return [held[k] for k in range(n)]


def beside(value, axis):
    return shift(value, axis, -1), shift(value, axis, 1)


def square(value, right, left, axis):
    far = jnp.stack([shift(left[0], axis, 1), shift(right[1], axis, -1)])
    return [value, right, far, left]


def over_row(value, hold=None):
    across = shift(value, "xl", 1)
    near = shift(value, "core", 1)
    if hold is not None:
        across = after(across, hold)
    return [value, near, across, shift(across, "core", 1)]


def tdot(left, right):
    return lax.dot_general(
        left, right, (((0,), (0,)), ((), ())), preferred_element_type=jnp.float32
    )


def pair_tdot(left, right):
    k, m = right.shape[0], left.shape[-1]
    return tdot(left[0].reshape(k, m), right), tdot(left[1].reshape(k, m), right)


def added(one, two):
    return one[0] + two[0], one[1] + two[1]


def combined(first, second):
    half = first.shape[1] // 2
    return first[:, :half] - second[:, half:], first[:, half:] + second[:, :half]


def body(linv_t, rhs_top, factor_t, rhs_rest):
    r = 2 * lax.axis_index("xl") + lax.axis_index("core")
    y, xh = lax.axis_index("y"), lax.axis_index("xh")
    wide = 2 * rhs_top.shape[2]
    scope = jax.named_scope

    def both_halves(own, other):
        low = jnp.where(xh == 0, own, other)
        return jnp.stack([low, jnp.where(xh == 0, other, own)], axis=1)

    def near_y(value):
        moved = [value, shift(value, "y", -1), shift(value, "y", 2), shift(value, "y", 1)]
        return laid_out(moved, 1, row_distance)

    with scope("panel_x"):
        own = jnp.concatenate([linv_t, factor_t], axis=2)
        both = both_halves(own, shift(own, "xh", 1))
    n_l = linv_t.shape[2]
    a_cols = jnp.concatenate([both[..., :L_A], both[..., n_l : n_l + F_A]], axis=3)
    b_cols = jnp.concatenate([both[..., L_A:n_l], both[..., n_l + F_A :]], axis=3)

    top = jnp.concatenate([rhs_top[0], rhs_top[1]], axis=1)
    top_high = lax.reduce_precision(top, 8, 7)
    top_low = (top - top_high).astype(jnp.bfloat16)
    with scope("top_row"):
        top_high = after(top_high.astype(jnp.bfloat16), both)

    with scope("b_z"):
        line = lax.all_gather(b_cols, "z", axis=2, tiled=True)
    with scope("a_y"):
        near = near_y(a_cols)
    own_l, own_f = line[..., : n_l - L_A], line[..., n_l - L_A :]
    with scope("inverse_b_y"):
        right_l, left_l = beside(own_l, "y")
    with scope("inverse_a_z"):
        holds = {3: (line,), 4: (right_l, left_l)}
        ring_l = ring(near[..., :L_A], "z", True, holds)
        a_l = laid_out(ring_l, 3, along_z)
    with scope("top_row"):
        tops = jnp.stack(over_row(top_high, ring_l[2]))
    with scope("inverse_b_y"):
        b_l = square(own_l, right_l, left_l, "y")
    with scope("factor_a_z"):
        a_f = lax.all_gather(after(near[..., L_A:], line), "z", axis=3, tiled=True)
    with scope("factor_b_y"):
        own_f = after(own_f, right_l, left_l)
        b_f = square(own_f, *beside(own_f, "y"), "y")

    place = [r ^ jnp.mod(y + o, 4) for o in range(4)]

    def times_a(whole, right):
        return pair_tdot(whole, right.reshape(-1, wide))

    def times_b(pieces, right):
        sums = None
        for o in (0, 1, 3, 2):
            mine = lax.dynamic_index_in_dim(right, place[o], 0, keepdims=False)
            term = pair_tdot(pieces[o], mine.reshape(-1, wide))
            sums = term if sums is None else added(sums, term)
        return sums

    def sent(parts, hold=None):
        half = jnp.concatenate([p.astype(jnp.bfloat16) for p in parts], axis=1)
        return jnp.stack(over_row(half, hold))

    with scope("solve_a"):
        own = pair_tdot(a_l[:, 0], top_low)
        solved_a = combined(*added(times_a(a_l, tops), own))
    with scope("solved_a_row"):
        half_a = sent(solved_a)
    with scope("solve_b"):
        own = lax.select_n(jnp.mod(r - y, 4), *b_l)
        own = pair_tdot(own, top_low)
        solved_b = combined(*added(times_b(b_l, tops), own))
    with scope("solved_b_row"):
        half_b = sent(solved_b, a_f)
    solved = jnp.stack([jnp.concatenate([solved_a[c], solved_b[c]], axis=0) for c in range(2)])
    halves = jnp.stack([half_a, half_b], axis=1)

    with scope("update_a"):
        update_a = combined(*times_a(a_f, halves))
    with scope("update_b"):
        update_b = combined(*times_b(b_f, halves))
    rest = [
        [rhs_rest[c, :F_A] - update_a[c], rhs_rest[c, F_A:] - update_b[c]] for c in range(2)
    ]
    return solved, jnp.stack([jnp.concatenate(part, axis=0) for part in rest])


def solution(mesh):
    axes = ("xl", "core", "y", "xh", "z")
    finer = Mesh(mesh.devices.reshape(2, 2, 4, 2, 8), axes)
    row, ang = axes[:2], axes[2:]
    placed = (P(None, ang, row), P(None, row, ang), P(None, ang, row), P(None, row, ang))
    return jax.shard_map(
        body,
        mesh=finer,
        in_specs=placed,
        out_specs=(P(None, row, ang), P(None, row, ang)),
        check_vma=False,
    )
```

```python
import math

import jax
import jax.numpy as jnp
from jax import lax
from jax.experimental import pallas as pl
from jax.experimental.pallas import tpu as pltpu
from jax.sharding import Mesh
from jax.sharding import PartitionSpec as P

L_A = 256
F_A = 512


def gated(values, *earlier):
    n = len(values)

    def kernel(*refs):
        pass

    anywhere = pl.BlockSpec(memory_space=pl.ANY)
    return pl.pallas_call(
        kernel,
        out_shape=[jax.ShapeDtypeStruct(v.shape, v.dtype) for v in values],
        in_specs=[anywhere] * (n + len(earlier)),
        out_specs=[anywhere] * n,
        input_output_aliases={i: i for i in range(n)},
        cost_estimate=pl.CostEstimate(flops=0, bytes_accessed=0, transcendentals=0),
    )(*values, *earlier)


def after(value, *earlier):
    return lax.optimization_barrier((value, *earlier))[0]


def shift(value, axis, step):
    n = lax.axis_size(axis)
    return lax.ppermute(value, axis, [(i, (i + step) % n) for i in range(n)])


def laid_out(pieces, dim, places):
    first = pieces[0]
    shape = (*first.shape[:dim], len(pieces), *first.shape[dim:])
    lead = (slice(None),) * dim

    def kernel(*refs):
        out = refs[len(pieces)]
        for i, at in enumerate(places()):
            out[(*lead, at)] = refs[i][...]

    size = 2 * math.prod(shape) * first.dtype.itemsize
    return pl.pallas_call(
        kernel,
        out_shape=jax.ShapeDtypeStruct(shape, first.dtype),
        in_specs=[pl.BlockSpec(memory_space=pltpu.VMEM)] * len(pieces),
        out_specs=pl.BlockSpec(memory_space=pltpu.VMEM),
        compiler_params=pltpu.CompilerParams(vmem_limit_bytes=16 << 20),
        cost_estimate=pl.CostEstimate(flops=0, bytes_accessed=size, transcendentals=0),
    )(*pieces)


def row_distance():
    r = 2 * lax.axis_index("xl") + lax.axis_index("core")
    y = lax.axis_index("y")
    return [r ^ lax.rem(y + o, 4) for o in range(4)]


def along_z():
    z = lax.axis_index("z")
    return [lax.rem(z + o, 8) for o in range(8)]


def ring(value, axis, far_up, holds=None):
    n = lax.axis_size(axis)
    held = {0: value}
    for k in range(1, n // 2 + 1):
        up, down = held[(n - k + 1) % n], held[k - 1]
        if k > 1:
            extra = () if holds is None else holds.get(k, ())
            up, down = lax.optimization_barrier((up, down, *extra))[:2]
        if k < n // 2 or far_up:
            held[n - k] = shift(up, axis, 1)
        if k < n // 2 or not far_up:
            held[k] = shift(down, axis, -1)
    return [held[k] for k in range(n)]


def beside(value, axis):
    return shift(value, axis, -1), shift(value, axis, 1)


def square(value, right, left, axis):
    far = shift(left[0], axis, 1), shift(right[1], axis, -1)
    return [value, right, far, left]


def over_row(value, hold=None):
    across = shift(value, "xl", 1)
    near = shift(value, "core", 1)
    if hold is not None:
        across = after(across, hold)
    return [value, near, across, shift(across, "core", 1)]


def tdot(left, right):
    return lax.dot_general(
        left, right, (((0,), (0,)), ((), ())), preferred_element_type=jnp.float32
    )


def pair_tdot(left, right):
    k, m = right.shape[0], left[0].shape[-1]
    return tdot(left[0].reshape(k, m), right), tdot(left[1].reshape(k, m), right)


def added(one, two):
    return one[0] + two[0], one[1] + two[1]


def combined(first, second):
    half = first.shape[1] // 2
    return first[:, :half] - second[:, half:], first[:, half:] + second[:, :half]


def body(linv_t, rhs_top, factor_t, rhs_rest):
    r = 2 * lax.axis_index("xl") + lax.axis_index("core")
    y, xh = lax.axis_index("y"), lax.axis_index("xh")
    wide = 2 * rhs_top.shape[2]
    scope = jax.named_scope

    def both_halves(own, other):
        low = jnp.where(xh == 0, own, other)
        return jnp.stack([low, jnp.where(xh == 0, other, own)], axis=1)

    def near_y(value):
        moved = [value, shift(value, "y", -1), shift(value, "y", 2), shift(value, "y", 1)]
        return laid_out(moved, 1, row_distance)

    with scope("panel_x"):
        own = jnp.concatenate([linv_t, factor_t], axis=2)
        both = both_halves(own, shift(own, "xh", 1))
    n_l = linv_t.shape[2]
    a_cols = jnp.concatenate([both[..., :L_A], both[..., n_l : n_l + F_A]], axis=3)
    b_cols = jnp.concatenate([both[..., L_A:n_l], both[..., n_l + F_A :]], axis=3)

    top = jnp.concatenate([rhs_top[0], rhs_top[1]], axis=1)
    top_high = lax.reduce_precision(top, 8, 7)
    top_low = (top - top_high).astype(jnp.bfloat16)
    with scope("top_row"):
        top_high = after(top_high.astype(jnp.bfloat16), both)

    with scope("b_z"):
        line = lax.all_gather(b_cols, "z", axis=2, tiled=True)
    with scope("a_y"):
        near = near_y(a_cols)
    own_l, own_f = line[..., : n_l - L_A], line[..., n_l - L_A :]
    with scope("inverse_b_y"):
        right_l, left_l = beside(own_l, "y")
    with scope("inverse_a_z"):
        holds = {3: (line,), 4: (right_l, left_l)}
        ring_l = ring(near[..., :L_A], "z", True, holds)
        a_l = laid_out(ring_l, 3, along_z)
    with scope("top_row"):
        tops = jnp.stack(over_row(top_high, ring_l[2]))
    with scope("inverse_b_y"):
        b_l = square(own_l, right_l, left_l, "y")
    with scope("factor_a_z"):
        a_f = lax.all_gather(after(near[..., L_A:], line), "z", axis=3, tiled=True)
    with scope("factor_b_y"):
        own_f = after(own_f, right_l, left_l)
        b_f = square(own_f, *beside(own_f, "y"), "y")

    place = [r ^ jnp.mod(y + o, 4) for o in range(4)]

    def times_a(whole, right):
        return pair_tdot(whole, right.reshape(-1, wide))

    def times_b(pieces, right, *earlier):
        sums = None
        for o in (0, 1, 3, 2):
            mine = lax.dynamic_index_in_dim(right, place[o], 0, keepdims=False)
            piece = pieces[o]
            if o == 2 and earlier:
                corners = [v[:8, :128] for v in (*sums, *earlier)]
                piece = tuple(gated(piece, *corners))
            term = pair_tdot(piece, mine.reshape(-1, wide))
            sums = term if sums is None else added(sums, term)
        return sums

    def sent(parts, hold=None):
        half = jnp.concatenate([p.astype(jnp.bfloat16) for p in parts], axis=1)
        return jnp.stack(over_row(half, hold))

    with scope("solve_a"):
        own = pair_tdot(a_l[:, 0], top_low)
        solved_a = combined(*added(times_a(a_l, tops), own))
    with scope("solved_a_row"):
        half_a = sent(solved_a)
    with scope("solve_b"):
        own = tuple(
            lax.select_n(jnp.mod(r - y, 4), *[piece[c] for piece in b_l]) for c in range(2)
        )
        own = pair_tdot(own, top_low)
        solved_b = combined(*added(times_b(b_l, tops), own))
    with scope("solved_b_row"):
        half_b = sent(solved_b, a_f)
    solved = jnp.stack([jnp.concatenate([solved_a[c], solved_b[c]], axis=0) for c in range(2)])
    halves = jnp.stack([half_a, half_b], axis=1)

    with scope("update_a"):
        sums_a = times_a(a_f, halves)
        update_a = combined(*sums_a)
    with scope("update_b"):
        update_b = combined(*times_b(b_f, halves, *sums_a))
    rest = [
        [rhs_rest[c, :F_A] - update_a[c], rhs_rest[c, F_A:] - update_b[c]] for c in range(2)
    ]
    return solved, jnp.stack([jnp.concatenate(part, axis=0) for part in rest])


def solution(mesh):
    axes = ("xl", "core", "y", "xh", "z")
    finer = Mesh(mesh.devices.reshape(2, 2, 4, 2, 8), axes)
    row, ang = axes[:2], axes[2:]
    placed = (P(None, ang, row), P(None, row, ang), P(None, ang, row), P(None, row, ang))
    return jax.shard_map(
        body,
        mesh=finer,
        in_specs=placed,
        out_specs=(P(None, row, ang), P(None, row, ang)),
        check_vma=False,
    )
```
